256 devices in a mesh: section: 16 (over z_hi, x), dp: 4 (over y), tensor: 4 (over z_lo, core).
Axes of the slice: x: 4, y: 4, z: 8 (z_hi: 4, z_lo: 2; z = z_hi * 2 + z_lo), core: 2. Of those that a mesh axis runs over, the one named last changes fastest.
Arguments:
- context: bfloat16 [16, 1024, 3072], P('section', 'dp', 'tensor'), may hold values from -6 to 6
- out_weight: bfloat16 [16, 6144, 3072], P('section', 'dp', 'tensor'), may hold values from -0.109375 to 0.109375
- residual: bfloat16 [16, 1024, 6144], P('section', 'dp', 'tensor'), may hold values from -6 to 6
- send_table: bfloat16 [16, 16, 128, 6144], P('section', 'dp', None, 'tensor'), may hold values from -6 to 6
- recv_table: bfloat16 [16, 16, 128, 6144], P('section', 'dp', None, 'tensor'), may hold values from -52 to 52
- sample_ids: int32 [8], P('dp'), may hold values from 0 to 3, as said below
- norm_gain: float32 [16, 6144], P('section', 'tensor'), may hold values from 0.5 to 1.5
- norm_bias: float32 [16, 6144], P('section', 'tensor'), may hold values from -3 to 3
- cotangent: bfloat16 [16, 1024, 6144], P('section', 'dp', 'tensor'), may hold values from -5.2 to 5.2
Outputs:
- refreshed: bfloat16 [16, 1024, 6144], P('section', 'dp', 'tensor')
- normed: bfloat16 [16, 1024, 6144], P('section', 'dp', 'tensor')
- weight_grad: bfloat16 [16, 6144, 3072], P('section', 'dp', 'tensor')
- context_grad: bfloat16 [16, 1024, 3072], P('section', 'dp', 'tensor')
The draws below stay inside these ranges and needn't reach their ends.
Inputs may be any that keep to these rules, and one draw needn't show every extreme that they name: `sample_ids`: within the 2 entries of one replica the ids are distinct.
All inputs are finite; a program needn't handle non-finite values. Where the reference program divides by a largest or mean magnitude, that divisor is 1e-20 or more.
Results may differ from the reference program's by a relative error of at most 0.015.
Values may be sent and summed in bfloat16 or wider, within the bound.
No kernel may reach another device: no remote copies, remote signals or barrier semaphores. Data moves between devices by JAX's collectives and lax.ppermute only.
A program may use at most 128 MiB of HBM per device.

```python
import math
import jax
import jax.numpy as jnp
from jax import lax

D = 6144
BLK = 128
SLEN = 128
TOK_DEV = 256
HC = 3072
MB = 2
SAMP_DEV = 4
SECTIONS = 16
TOKENS = 1024
SAMPLES = 16
NBATCH = 8
N_DP = 4
N_TENSOR = 4


def draw_sample_ids(key, part):
    key = jax.random.fold_in(key, 5)
    replicas = NBATCH // MB
    subkeys = jax.random.split(key, replicas + 1)
    orders = jax.vmap(lambda sub_key: jax.random.permutation(sub_key, SAMP_DEV))(subkeys[:replicas])
    drawn_ints = jax.random.randint(subkeys[replicas], (4,), 0, 1 << 20)
    high_rep = drawn_ints[0] % replicas
    low_rep = (high_rep + 1 + drawn_ints[1] % (replicas - 1)) % replicas
    high_slot = drawn_ints[2] % MB
    low_slot = drawn_ints[3] % MB

    def place(ranking, target, slot_index):
        position = jnp.argmax(ranking == target)
        displaced = ranking[slot_index]
        return ranking.at[position].set(displaced).at[slot_index].set(target)
    lifted = jax.vmap(lambda ranking: place(ranking, SAMP_DEV - 1, high_slot))(orders)
    lowered = jax.vmap(lambda ranking: place(ranking, 0, low_slot))(orders)
    rep_index = jnp.arange(replicas)[:, None]
    orders = jnp.where(rep_index == high_rep, lifted, jnp.where(rep_index == low_rep, lowered, orders))
    return orders[:, :MB].reshape(NBATCH).astype(jnp.int32)


def draw_recv_table(key, part):
    key = jax.random.fold_in(key, 7)
    subkeys = jax.random.split(key, 3)
    full_shape = (SECTIONS, SAMPLES, SLEN, D)
    jitter = jnp.exp(jax.random.uniform(subkeys[1], (D,), jnp.float32, -0.35, 0.35))
    column_scale = 0.3 * 10.0 ** (jnp.arange(D, dtype=jnp.float32) / D) * jitter
    base = jnp.clip(jax.random.normal(subkeys[0], full_shape, jnp.float32), -4.0, 4.0)
    row_scale = jnp.exp(jax.random.uniform(subkeys[2], (SECTIONS, SAMPLES, SLEN, 1), jnp.float32, math.log(0.3), math.log(3.0)))
    return (base * row_scale * column_scale).astype(jnp.bfloat16)


def draw_cotangent(key, part):
    key = jax.random.fold_in(key, 9)
    subkeys = jax.random.split(key, 3)
    full_shape = (SECTIONS, TOKENS, D)
    jitter = jnp.exp(jax.random.uniform(subkeys[1], (D,), jnp.float32, -0.35, 0.35))
    column_scale = 0.03 * 10.0 ** (jnp.arange(D, dtype=jnp.float32) / D) * jitter
    base = jnp.clip(jax.random.normal(subkeys[0], full_shape, jnp.float32), -4.0, 4.0)
    row_scale = jnp.exp(jax.random.uniform(subkeys[2], (SECTIONS, TOKENS, 1), jnp.float32, math.log(0.3), math.log(3.0)))
    return (base * row_scale * column_scale).astype(jnp.bfloat16)


def steps_of(rng, extent, shards, smallest, high):
    def one(dim, parts):
        draws = jax.random.uniform(jax.random.fold_in(jax.random.fold_in(rng, 6), dim), (parts,), jnp.float32, smallest / len(shards), high / len(shards))
        return jnp.repeat(jnp.exp(draws), extent[dim] // parts).reshape((-1,) + (1,) * (len(extent) - dim - 1))

    level = one(*shards[0])
    for cut in shards[1:]:
        level = level * one(*cut)
    return level


def centred(own_key, extent, deviation, reach, cuts=(), held_as=jnp.bfloat16):
    values = deviation * jax.random.normal(own_key, extent, jnp.float32)
    if cuts:
        values = values * steps_of(own_key, extent, cuts, -0.22, 0.18)
    return jnp.clip(values, -reach, reach).astype(held_as)


def setup_inputs(seed: int = 0) -> dict:
    splits = jax.random.split(jax.random.key(seed), 10)
    return {
        "context": centred(splits[0], (SECTIONS, TOKENS, HC), 1.0, 6.0, ((0, 16), (1, 4), (2, 4))),
        "out_weight": centred(splits[1], (SECTIONS, D, HC), HC ** -0.5, 0.109375, ((0, 16), (1, 4), (2, 4))),
        "residual": centred(splits[2], (SECTIONS, TOKENS, D), 1.0, 6.0, ((0, 16), (1, 4), (2, 4))),
        "send_table": centred(splits[3], (SECTIONS, SAMPLES, SLEN, D), 1.0, 6.0, ((0, 16), (1, 4), (3, 4))),
        "recv_table": draw_recv_table(jax.random.fold_in(splits[9], 71), 0),
        "sample_ids": draw_sample_ids(jax.random.fold_in(splits[9], 71), 0),
        "norm_gain": jnp.clip(1.0 + 0.1 * jax.random.normal(splits[6], (SECTIONS, D), jnp.float32), 0.5, 1.5),
        "norm_bias": centred(splits[7], (SECTIONS, D), 0.5, 3.0, ((0, 16), (1, 4)), jnp.float32),
        "cotangent": draw_cotangent(jax.random.fold_in(splits[9], 71), 0),
    }


def quantize(values):
    count_rows, count_cols = values.shape
    blocks = values.reshape(count_rows, count_cols // BLK, BLK)
    scales = (lax.optimization_barrier(jnp.max(jnp.abs(blocks), axis=2)) + 1e-06).astype(jnp.bfloat16)
    coded = (blocks / scales.astype(jnp.float32)[:, :, None]).astype(jnp.bfloat16)
    return (coded.reshape(count_rows, count_cols), scales)

def dequantize(coded, scales):
    count_rows, count_cols = coded.shape
    blocks = coded.astype(jnp.float32).reshape(count_rows, count_cols // BLK, BLK)
    return (blocks * scales.astype(jnp.float32)[:, :, None]).reshape(count_rows, count_cols)

def sample_rows(table, sample_ids):
    stored_index = sample_ids + jnp.arange(NBATCH, dtype=jnp.int32) // MB * SAMP_DEV
    return table[stored_index.astype(jnp.int32)].reshape(TOKENS, D)

def reference(context, out_weight, residual, send_table, recv_table, sample_ids, norm_gain, norm_bias, cotangent):

    def encode_section(operands):
        ctx_section, weight_section, resid_section, table_section = operands
        ctx_groups = ctx_section.astype(jnp.float32).reshape(TOKENS, N_TENSOR, HC // N_TENSOR)
        weight_groups = weight_section.astype(jnp.float32).reshape(D, N_TENSOR, HC // N_TENSOR)
        partials = jnp.einsum('tgk,dgk->gtd', ctx_groups, weight_groups).astype(jnp.bfloat16)
        partials = lax.optimization_barrier(partials)
        boundary = resid_section.astype(jnp.float32) + lax.optimization_barrier(jnp.sum(partials.astype(jnp.float32), axis=0))
        delta = boundary - sample_rows(table_section, sample_ids).astype(jnp.float32)
        return quantize(delta)
    coded, scales = lax.map(encode_section, (context, out_weight, residual, send_table))
    arrived_codes = jnp.roll(coded, 1, axis=0)
    arrived_scales = jnp.roll(scales, 1, axis=0)
    received = jax.vmap(lambda table_section: sample_rows(table_section, sample_ids))(recv_table)
    refreshed = (received.astype(jnp.float32) + jax.vmap(dequantize)(arrived_codes, arrived_scales)).astype(jnp.bfloat16)
    row_vals = refreshed.astype(jnp.float32)
    row_mean = lax.optimization_barrier(jnp.sum(row_vals, axis=2, keepdims=True)) / D
    variance = lax.optimization_barrier(jnp.sum(row_vals * row_vals, axis=2, keepdims=True)) / D - row_mean * row_mean
    inverse = lax.rsqrt(variance + 1e-05)
    normalized = (row_vals - row_mean) * inverse
    normed = (normalized * norm_gain[:, None, :] + norm_bias[:, None, :]).astype(jnp.bfloat16)
    scaled_grad = cotangent.astype(jnp.float32) * norm_gain[:, None, :]
    grad_mean = lax.optimization_barrier(jnp.sum(scaled_grad, axis=2, keepdims=True)) / D
    grad_proj = lax.optimization_barrier(jnp.sum(scaled_grad * normalized, axis=2, keepdims=True)) / D
    grad_in = inverse * (scaled_grad - grad_mean - normalized * grad_proj)
    grad_codes, grad_scales = jax.vmap(quantize)(grad_in)
    returned_codes = jnp.roll(grad_codes, -1, axis=0)
    returned_scales = jnp.roll(grad_scales, -1, axis=0)
    grad_act = jax.vmap(dequantize)(returned_codes, returned_scales).astype(jnp.bfloat16)

    def weight_section_grads(operands):
        grad_section, ctx_section, weight_section = operands
        grad_rep = grad_section.reshape(N_DP, TOK_DEV, D)
        ctx_rep = ctx_section.reshape(N_DP, TOK_DEV, HC)
        running = jnp.zeros((D, HC), jnp.float32)
        for replica in range(N_DP):
            term = jnp.dot(grad_rep[replica].T, ctx_rep[replica], preferred_element_type=jnp.float32).astype(jnp.bfloat16)
            term = lax.optimization_barrier(term)
            running = running + term.astype(jnp.float32)
        ctx_grad = jnp.dot(grad_section, weight_section, preferred_element_type=jnp.float32).astype(jnp.bfloat16)
        return (running.astype(jnp.bfloat16), ctx_grad)
    weight_grad, context_grad = lax.map(weight_section_grads, (grad_act, context, out_weight))
    return (refreshed, normed, weight_grad, context_grad)
```

```python
import functools
import jax
import jax.numpy as jnp
from jax import lax
from jax.experimental import pallas as pl
from jax.experimental.pallas import tpu as pltpu
from jax.sharding import PartitionSpec as P

BLK = 128
ROWS = 128
GROUP = 16
RING = 4
ALL = ("section", "dp", "tensor")
F32 = jnp.float32
BF16 = jnp.bfloat16
LAST = (((1,), (1,)), ((), ()))
FIRST = (((0,), (0,)), ((), ()))
PLAIN = (((1,), (0,)), ((), ()))


def params(mib=32):
    return pltpu.CompilerParams(vmem_limit_bytes=mib * 1024 * 1024)


def cost(flops, nbytes):
    return pl.CostEstimate(flops=flops, bytes_accessed=nbytes, transcendentals=0)


def crossed(x, k, axis="tensor"):
    n = lax.axis_size(axis)
    return lax.ppermute(x, axis, [(i, i ^ k) for i in range(n)])


def after(x, done):
    return x if done is None else lax.optimization_barrier((x, done))[0]


def added(*terms):
    return sum(v.astype(F32) for v in terms).astype(BF16)


def coded(values):
    largest = jnp.max(jnp.abs(values), axis=1, keepdims=True)
    scale = (jnp.broadcast_to(largest, values.shape) + 1e-06).astype(BF16).astype(F32)
    code = (values / scale).astype(BF16).astype(F32)
    return code * scale


def whole(shape):
    return pl.BlockSpec(shape, lambda *_: (0,) * len(shape))


def head_kernel(a00, a01, a10, a11, mine_ref, other_ref, p0, p1):
    prod = lax.dot_general(
        jnp.concatenate([a00[...], a10[...]], axis=0), mine_ref[...], LAST, preferred_element_type=F32
    ) + lax.dot_general(
        jnp.concatenate([a01[...], a11[...]], axis=0), other_ref[...], LAST, preferred_element_type=F32
    )
    rows = p0.shape[0]
    p0[...] = prod[:rows].astype(BF16)
    p1[...] = prod[rows:].astype(BF16)


def head(blocks, weight, other):
    feats, width = weight.shape
    rows = blocks[0].shape[0]
    tile = 256
    return pl.pallas_call(
        head_kernel,
        grid=(feats // tile,),
        in_specs=[whole((rows, width))] * 4 + [pl.BlockSpec((tile, width), lambda j: (j, 0))] * 2,
        out_specs=[pl.BlockSpec((rows, tile), lambda j: (0, j))] * 2,
        out_shape=[jax.ShapeDtypeStruct((rows, feats), BF16)] * 2,
        compiler_params=params(),
        cost_estimate=cost(8 * rows * width * feats, 4 * (feats * width + rows * (2 * width + feats))),
        name="head",
    )(*blocks, weight, other)


def pick_kernel(ids, table_ref, out_ref):
    out_ref[...] = table_ref[0]


def pick(ids, table):
    cols = table.shape[2]
    return pl.pallas_call(
        pick_kernel,
        grid_spec=pltpu.PrefetchScalarGridSpec(
            num_scalar_prefetch=1,
            grid=(ids.shape[0],),
            in_specs=[pl.BlockSpec((1, ROWS, cols), lambda b, ids: (ids[b], 0, 0))],
            out_specs=pl.BlockSpec((ROWS, cols), lambda b, ids: (b, 0)),
        ),
        out_shape=jax.ShapeDtypeStruct((ids.shape[0] * ROWS, cols), BF16),
        compiler_params=params(),
        cost_estimate=cost(1, ids.shape[0] * ROWS * cols * 4),
        name="pick",
    )(ids, table)


def sums_kernel(ids, y0, y1, res_ref, table_ref, recv_ref, cot_ref, gain_ref, out_ref, delta_ref, stat_ref, held):
    rows, cols = out_ref.shape
    for r in range(0, rows, GROUP):
        total = [jnp.zeros((GROUP, BLK), F32)] * 4
        for c in range(0, cols, BLK):
            at = (slice(r, r + GROUP), slice(c, c + BLK))
            boundary = res_ref[at].astype(F32) + (y0[at].astype(F32) + y1[at].astype(F32))
            delta = coded(boundary - table_ref[0, at[0], at[1]].astype(F32)).astype(BF16)
            delta_ref[at] = delta
            fresh = (recv_ref[at].astype(F32) + delta.astype(F32)).astype(BF16)
            out_ref[at] = fresh
            x = fresh.astype(F32)
            g = cot_ref[at].astype(F32) * gain_ref[:, at[1]]
            for i, v in enumerate((x, x * x, g, g * x)):
                total[i] = total[i] + v
        for i in range(4):
            held[i, r : r + GROUP, :] = total[i]
    for i in range(4):
        stat_ref[i : i + 1, :] = jnp.sum(held[i].T, axis=0, keepdims=True)
    stat_ref[4:8, :] = jnp.zeros((4, rows), F32)


def sums(ids, y0, y1, residual, table, recv, cot, gain):
    rows, cols = cot.shape
    chunk = pl.BlockSpec((ROWS, cols), lambda b, ids: (b, 0))
    return pl.pallas_call(
        sums_kernel,
        grid_spec=pltpu.PrefetchScalarGridSpec(
            num_scalar_prefetch=1,
            grid=(rows // ROWS,),
            in_specs=[chunk, chunk, chunk]
            + [pl.BlockSpec((1, ROWS, cols), lambda b, ids: (ids[b], 0, 0))]
            + [chunk, chunk, whole((1, cols))],
            out_specs=[chunk, chunk, pl.BlockSpec((8, ROWS), lambda b, ids: (b, 0))],
            scratch_shapes=[pltpu.VMEM((4, ROWS, BLK), F32)],
        ),
        out_shape=[
            jax.ShapeDtypeStruct((rows, cols), BF16),
            jax.ShapeDtypeStruct((rows, cols), BF16),
            jax.ShapeDtypeStruct((rows // ROWS * 8, ROWS), F32),
        ],
        compiler_params=params(),
        cost_estimate=cost(rows * cols * 20, rows * cols * 14),
        name="sums",
    )(ids, y0, y1, residual, table, recv, cot, gain)


def moments(stat, held):
    rows = held.shape[1]
    mean = stat[0:1]
    inverse = lax.rsqrt(stat[1:2] - mean * mean + 1e-05)
    grad_mean = stat[2:3]
    proj = (stat[3:4] - mean * grad_mean) * inverse
    for i, v in enumerate((mean, inverse, grad_mean, proj)[: held.shape[0]]):
        held[i] = jnp.broadcast_to(v, (rows, rows)).T


def norm_kernel(full, s0, s1, s2, s3, x_ref, cot_ref, gain_ref, stat_ref, out_ref, held):
    rows, cols = x_ref.shape
    stat_ref[...] = (s0[...] + s1[...] + s2[...] + s3[...]) / full
    moments(stat_ref[...], held)
    for r in range(0, rows, GROUP):
        mean, inverse, grad_mean, proj = (held[i, r : r + GROUP, :] for i in range(4))
        for c in range(0, cols, BLK):
            at = (slice(r, r + GROUP), slice(c, c + BLK))
            normalized = (x_ref[at].astype(F32) - mean) * inverse
            grad = cot_ref[at].astype(F32) * gain_ref[:, at[1]] - grad_mean - normalized * proj
            out_ref[at] = coded(inverse * grad).astype(BF16)


def norm(full, stats, x, cot, gain):
    rows, cols = x.shape
    chunk = pl.BlockSpec((ROWS, cols), lambda b: (b, 0))
    stat = pl.BlockSpec((8, ROWS), lambda b: (b, 0))
    return pl.pallas_call(
        functools.partial(norm_kernel, full),
        grid=(rows // ROWS,),
        in_specs=[stat] * 4 + [chunk, chunk, whole((1, cols))],
        out_specs=[stat, chunk],
        out_shape=[
            jax.ShapeDtypeStruct(stats[0].shape, F32),
            jax.ShapeDtypeStruct((rows, cols), BF16),
        ],
        scratch_shapes=[pltpu.VMEM((4, ROWS, ROWS), F32)],
        compiler_params=params(),
        cost_estimate=cost(rows * cols * 20, rows * cols * 6),
        name="norm",
    )(*stats, x, cot, gain)


def finish_kernel(ids, delta_ref, table_ref, stat_ref, gain_ref, bias_ref, fresh_ref, norm_ref, held):
    moments(stat_ref[...], held)
    rows, cols = fresh_ref.shape
    for r in range(0, rows, GROUP):
        mean, inverse = (held[i, r : r + GROUP, :] for i in range(2))
        for c in range(0, cols, BLK):
            at = (slice(r, r + GROUP), slice(c, c + BLK))
            received = table_ref[0, at[0], at[1]].astype(F32)
            fresh = (received + delta_ref[at].astype(F32)).astype(BF16)
            fresh_ref[at] = fresh
            normalized = (fresh.astype(F32) - mean) * inverse
            norm_ref[at] = (normalized * gain_ref[:, at[1]] + bias_ref[:, at[1]]).astype(BF16)


def finish(ids, delta, table, stat, gain, bias):
    rows, cols = delta.shape
    chunk = pl.BlockSpec((ROWS, cols), lambda b, ids: (b, 0))
    return pl.pallas_call(
        finish_kernel,
        grid_spec=pltpu.PrefetchScalarGridSpec(
            num_scalar_prefetch=1,
            grid=(rows // ROWS,),
            in_specs=[
                chunk,
                pl.BlockSpec((1, ROWS, cols), lambda b, ids: (ids[b], 0, 0)),
                pl.BlockSpec((8, ROWS), lambda b, ids: (b, 0)),
                whole((1, cols)),
                whole((1, cols)),
            ],
            out_specs=[chunk, chunk],
            scratch_shapes=[pltpu.VMEM((2, ROWS, ROWS), F32)],
        ),
        out_shape=[jax.ShapeDtypeStruct((rows, cols), BF16)] * 2,
        compiler_params=params(),
        cost_estimate=cost(rows * cols * 8, rows * cols * 8),
        name="finish",
    )(ids, delta, table, stat, gain, bias)


def back_kernel(place, g0, g1, g2, g3, w_ref, e0, e1, e2, e3, held):
    grads = jnp.concatenate([g[...] for g in (g0, g1, g2, g3)], axis=0)
    prod = lax.dot_general(grads, w_ref[...], PLAIN, preferred_element_type=F32).astype(BF16)
    held[...] = prod.reshape(held.shape)
    for d, e in enumerate((e0, e1, e2, e3)):
        e[...] = held[jnp.bitwise_xor(place[0], d % 2) * 2 + jnp.bitwise_xor(place[1], d // 2)]


def back(place, grads, weight):
    feats, width = weight.shape
    rows = grads[0].shape[0]
    tile = 256
    return pl.pallas_call(
        back_kernel,
        grid_spec=pltpu.PrefetchScalarGridSpec(
            num_scalar_prefetch=1,
            grid=(width // tile,),
            in_specs=[whole((rows, feats))] * 4 + [pl.BlockSpec((feats, tile), lambda j, place: (0, j))],
            out_specs=[pl.BlockSpec((rows, tile), lambda j, place: (0, j))] * 4,
            scratch_shapes=[pltpu.VMEM((4, rows, tile), BF16)],
        ),
        out_shape=[jax.ShapeDtypeStruct((rows, width), BF16)] * 4,
        compiler_params=params(),
        cost_estimate=cost(8 * rows * width * feats, 2 * (feats * width + 4 * rows * (width + feats))),
        name="back",
    )(place, *grads, weight)


def weights_kernel(count, *refs):
    grads, ctx, out_ref = refs[:count], refs[count : 2 * count], refs[-1]
    lhs = jnp.concatenate([g[...] for g in grads], axis=0)
    rhs = jnp.concatenate([c[...] for c in ctx], axis=0)
    out_ref[...] = lax.dot_general(lhs, rhs, FIRST, preferred_element_type=F32).astype(BF16)


def weights(grads, blocks):
    count = len(grads)
    rows, feats = grads[0].shape
    width = blocks[0].shape[1]
    tile = 256
    return pl.pallas_call(
        functools.partial(weights_kernel, count),
        grid=(feats // tile,),
        in_specs=[pl.BlockSpec((rows, tile), lambda j: (0, j))] * count + [whole((rows, width))] * count,
        out_specs=pl.BlockSpec((tile, width), lambda j: (j, 0)),
        out_shape=jax.ShapeDtypeStruct((feats, width), BF16),
        compiler_params=params(),
        cost_estimate=cost(2 * count * rows * width * feats, 2 * (feats * width + count * rows * (width + feats))),
        name="weights",
    )(*grads, *blocks)


def body(
    context,
    out_weight,
    residual,
    send_table,
    recv_table,
    sample_ids,
    norm_gain,
    norm_bias,
    cotangent,
):
    n_sec, n_dp, n_ten = (lax.axis_size(a) for a in ALL)
    ctx, weight = context[0], out_weight[0]
    def index(z, x, q, r):
        return ((z % (n_sec // RING) * RING + x % RING) * n_dp + q) * n_ten + r

    places = [
        (z, x, q, r)
        for z in range(n_sec // RING)
        for x in range(RING)
        for q in range(n_dp)
        for r in range(n_ten)
    ]

    def sent(x, place, inverse=False):
        pairs = [(index(*p), index(*place(*p))) for p in places]
        return lax.ppermute(x, ALL, [(b, a) for a, b in pairs] if inverse else pairs)

    def owner(q, r, k):
        return q ^ (r % 2 + 2 * (k ^ (r // 2)))

    def spread(x, k, inverse=False):
        return sent(x, lambda z, x, q, r: (z, x, owner(q, r, k), q), inverse)

    def fetch(x, k, o):
        return sent(x, lambda z, x, q, r: (z, x, owner(q, r, k), r ^ o), True)

    def passed(x, step):
        wrap = RING - 1 if step > 0 else 0
        return sent(x, lambda z, x, q, r: (z + step * (x == wrap), x + step, q, r))

    def along(x, step):
        return sent(x, lambda z, x, q, r: (z, x + step, q, r))

    def across(x, step, first):
        column = (RING - 1 if step > 0 else 0) if first else (0 if step > 0 else RING - 1)
        return sent(x, lambda z, x, q, r: (z + step * (x == column), x, q, r))

    t = lax.axis_index("tensor")
    place = jnp.stack([t % 2, t // 2]).astype(jnp.int32)

    other = crossed(weight, 1)
    cot = along(cotangent[0], -1)
    columns = [fetch(ctx, 1, 0), fetch(ctx, 1, 1), fetch(ctx, 0, 1)]
    columns.append(fetch(after(ctx, (other, columns[0])), 0, 0))
    recv = across(after(pick(sample_ids, recv_table[0]), other), -1, True)
    prods = head([columns[i] for i in (3, 2, 0, 1)], weight, other)
    rest = [crossed(v, 1) for v in (columns[2], columns[1])]
    prods, rest = lax.optimization_barrier((prods, rest))
    y = [spread(u, k) for k, u in enumerate(prods)]
    cot = across(cot, -1, False)
    recv = along(recv, -1)
    gain = passed(after(norm_gain, prods), -1)

    x, delta, stat = sums(sample_ids, *y, residual[0], send_table[0], recv, cot, gain)
    delta = passed(delta, 1)
    stats = [stat] + [crossed(stat, k) for k in range(1, 4)]
    full = float(n_ten * residual.shape[2])
    stat, grad = norm(full, stats, x, cot, gain)
    stat = passed(stat, 1)
    grads = [spread(grad, k, True) for k in (0, 1)]
    grads = grads + [crossed(v, 1) for v in grads]
    mine, *terms = back(place, grads, weight)
    came = [crossed(e, d, "dp") for d, e in enumerate(terms, 1)]
    weight_grad = weights(grads, [columns[3], columns[0], *rest])
    refreshed, normed = finish(sample_ids, delta, recv_table[0], after(stat, weight_grad), norm_gain, norm_bias)
    came, weight_grad = lax.optimization_barrier((came, weight_grad))
    ctx_grad = added(mine, *came)

    return (refreshed[None], normed[None], weight_grad[None], ctx_grad[None])


def solution(mesh):
    rows = P("section", "dp", "tensor")
    table = P("section", "dp", None, "tensor")
    line = P("section", "tensor")
    return jax.shard_map(
        body,
        mesh=mesh,
        in_specs=(rows, rows, rows, table, table, P("dp"), line, line, rows),
        out_specs=(rows, rows, rows, rows),
        check_vma=False,
    )
```
